32 devices in a mesh: row: 16 (over z, y, core), bundle: 2 (over x).
Axes of the slice: x: 2, y: 2, z: 4, core: 2. Of those that a mesh axis runs over, the one named last changes fastest.
Arguments:
- vectors: float32 [256, 32768], P('bundle', 'row'), may hold values from -6 to 6
- blocks: float32 [512, 64, 384], P('row'), may hold values from -0.30618622 to 0.30618622, as said below
- columns: int32 [512, 6], P('row'), may hold values from 0 to 511, as said below
- bounds: float32 [2], replicated, may hold values from -0.9 to 0.5, as said below
Outputs:
- basis: float32 [256, 32768], P(None, ('row', 'bundle'))
- factor: float32 [256, 256], replicated
The draws below stay inside these ranges and needn't reach their ends.
Inputs may be any that keep to these rules, and one draw needn't show every extreme that they name: Slot 0 of block row i is i itself; every block column of block row i lies within 32 block rows of i, counted cyclically over the 512 block rows, and a distance of exactly 32 occurs; columns of one block row may repeat. `blocks`: together with columns they make H symmetric. bounds[0] < 0 < bounds[1].
All inputs are finite; a program needn't handle non-finite values.
Results may differ from the reference program's by a relative error of at most 0.00011.
Values sent between devices are 32-bit elements; how exact they have to be, the bound alone decides.
A program may use at most 64 MiB of HBM per device.

```python
import jax
import jax.numpy as jnp
from jax import lax

BS = 64
SLOTS = 6
K = 256
BR_DEV = 32
NBR = 512
N = 32768


def pattern_tables(key):
    base = jax.random.fold_in(key, 101)
    rows = jnp.arange(NBR, dtype=jnp.int32)
    window = BR_DEV
    forward = []
    backward = []
    for pair_index in range(2):
        pair_key = jax.random.fold_in(base, pair_index)
        start = jax.random.randint(jax.random.fold_in(pair_key, 1), (), 0, window).astype(jnp.int32)
        turns = jax.random.randint(jax.random.fold_in(pair_key, 2), (NBR // window,), 1, window).astype(jnp.int32)
        position = jnp.mod(rows - start, NBR)
        which = position // window
        inner = position % window
        turn = turns[which]
        forward.append(jnp.mod(start + which * window + jnp.mod(inner + turn, window), NBR).astype(jnp.int32))
        backward.append(jnp.mod(start + which * window + jnp.mod(inner - turn, window), NBR).astype(jnp.int32))
    match_start = jax.random.randint(jax.random.fold_in(base, 7), (), 0, 2 * window).astype(jnp.int32)
    match_inner = jnp.mod(rows - match_start, NBR) % (2 * window)
    lower_half = match_inner < window
    partner = jnp.mod(rows + jnp.where(lower_half, window, -window), NBR).astype(jnp.int32)
    return (rows, forward, backward, partner, lower_half)


def draw_columns(key, part):
    rows, forward, backward, partner, lower_half = pattern_tables(key)
    return jnp.stack([rows, forward[0], backward[0], forward[1], backward[1], partner], axis=1).astype(jnp.int32)


def draw_blocks(key, part):
    rows, forward, backward, partner, lower_half = pattern_tables(key)
    sigma = (SLOTS * BS) ** (-0.5)
    raw_key = jax.random.fold_in(key, 211)
    raw = jnp.clip(jax.random.normal(raw_key, (NBR, SLOTS, BS, BS), jnp.float32), -6.0, 6.0) * sigma
    flip = lambda m: jnp.swapaxes(m, -1, -2)
    slot0 = 0.5 * (raw[:, 0] + flip(raw[:, 0]))
    slot1 = raw[:, 1]
    slot2 = flip(jnp.take(raw[:, 1], backward[0], axis=0))
    slot3 = raw[:, 3]
    slot4 = flip(jnp.take(raw[:, 3], backward[1], axis=0))
    slot5 = jnp.where(lower_half[:, None, None], raw[:, 5], flip(jnp.take(raw[:, 5], partner, axis=0)))
    stacked = jnp.stack([slot0, slot1, slot2, slot3, slot4, slot5], axis=1)
    return jnp.transpose(stacked, (0, 2, 1, 3)).reshape(NBR, BS, SLOTS * BS).astype(jnp.float32)


def draw_bounds(key, part):
    lower_end = jax.random.uniform(jax.random.fold_in(key, 31), (), jnp.float32, -0.9, -0.5)
    upper_end = jax.random.uniform(jax.random.fold_in(key, 37), (), jnp.float32, 0.1, 0.5)
    return jnp.stack([lower_end, upper_end]).astype(jnp.float32)


def shard_levels(rng, dims, shards, smallest, top_value):
    gain, own = 1.0, jax.random.fold_in(rng, 6)
    for dim, shards_of in shards:
        heights = jnp.exp(jax.random.uniform(jax.random.fold_in(own, dim), (shards_of,), jnp.float32, smallest / len(shards), top_value / len(shards)))
        gain = gain * jnp.repeat(heights, dims[dim] // shards_of).reshape([-1 if axis == dim else 1 for axis in range(len(dims))])
    return gain


def gaussian(stream_key, shape, spread, reach, shards=(), kind=jnp.bfloat16):
    drawn = spread * jax.random.normal(stream_key, shape, jnp.float32)
    if shards:
        drawn = drawn * shard_levels(stream_key, shape, shards, -0.22, 0.18)
    return jnp.clip(drawn, -reach, reach).astype(kind)


def setup_inputs(seed: int = 0) -> dict:
    splits = jax.random.split(jax.random.key(seed), 5)
    vectors = gaussian(splits[0], (K, N), 1.0, 6.0, ((0, 2), (1, 16)), jnp.float32)
    blocks = draw_blocks(jax.random.fold_in(splits[4], 71), 0)
    columns = draw_columns(jax.random.fold_in(splits[4], 71), 0)
    bounds = draw_bounds(jax.random.fold_in(splits[4], 71), 0)
    return {"vectors": vectors, "blocks": blocks, "columns": columns, "bounds": bounds}


def apply_operator(field, blocks, columns):
    width = field.shape[0]
    nblock = blocks.shape[0]
    field3 = field.reshape(width, nblock, BS)
    total = jnp.zeros((width, nblock, BS), jnp.float32)
    for slot in range(SLOTS):
        picked = jnp.take(field3, columns[:, slot], axis=1)
        piece = blocks[:, :, slot * BS:(slot + 1) * BS]
        total = total + jnp.einsum('iab,cib->cia', piece, picked, precision=lax.Precision.HIGHEST)
    return total.reshape(width, nblock * BS)

def reference(vectors, blocks, columns, bounds):
    center = (bounds[0] + bounds[1]) * 0.5
    half = (bounds[1] - bounds[0]) * 0.5
    first = (apply_operator(vectors, blocks, columns) - center * vectors) / half
    second = 2.0 * (apply_operator(first, blocks, columns) - center * first) / half - vectors
    filtered = 2.0 * (apply_operator(second, blocks, columns) - center * second) / half - first
    gram = jnp.dot(filtered.astype(jnp.float32), filtered.T.astype(jnp.float32), precision=lax.Precision.HIGHEST, preferred_element_type=jnp.float32)
    lower = jnp.linalg.cholesky(gram)
    basis = jax.scipy.linalg.solve_triangular(lower, filtered, lower=True)
    return (basis, lower.T)
```

```python
import functools

import jax
import jax.numpy as jnp
from jax import lax
from jax.experimental import pallas as pl
from jax.experimental.pallas import tpu as pltpu
from jax.sharding import PartitionSpec as P

MESH = pl.DeviceIdType.MESH
F32 = jnp.float32
BF16 = jnp.bfloat16
HIGHEST = lax.Precision.HIGHEST
VMEM_LIMIT = 56 * 1024 * 1024
PANEL = 64


def split(value):
    high = value.astype(BF16)
    return high, (value - high.astype(F32)).astype(BF16)


def filter_kernel(
    rows, bundles, cols_ref, bounds_ref, vec_ref, blocks_ref, stacked_ref, gram_ref,
    ablk, high, low, fields, halo, gram_in, halo_send, halo_recv, all_send, all_recv,
    gram_send, gram_recv,
):
    me = lax.axis_index("row")
    mine = lax.axis_index("bundle")
    br, bs = blocks_ref.shape[0], blocks_ref.shape[1]
    slots = cols_ref.shape[1]
    width = vec_ref.shape[0]
    total = br * rows
    right = lax.rem(me + 1, rows)
    left = lax.rem(me + rows - 1, rows)
    chunks = 4
    per = br // chunks

    row_bits = rows.bit_length() - 1
    bundle_bits = bundles.bit_length() - 1
    partners = []
    for bit in range(row_bits):
        mask = 1 << bit
        upper = lax.rem(lax.div(me, mask), 2)
        partners.append({"row": me + mask - 2 * mask * upper})
    for bit in range(bundle_bits):
        mask = 1 << bit
        upper = lax.rem(lax.div(mine, mask), 2)
        partners.append({"bundle": mine + mask - 2 * mask * upper})
    others = [{"bundle": lax.rem(mine + step, bundles)} for step in range(1, bundles)]

    barrier = pltpu.get_barrier_semaphore()
    greeted = [{"row": left}, {"row": right}] + partners + others
    for device in greeted:
        pl.semaphore_signal(barrier, inc=1, device_id=device, device_id_type=MESH)

    center = (bounds_ref[0] + bounds_ref[1]) * 0.5
    inverse = 1.0 / ((bounds_ref[1] - bounds_ref[0]) * 0.5)

    def halo_copies(step, chunk):
        part = pl.ds(chunk * per, per)
        return [
            pltpu.make_async_remote_copy(
                src_ref=fields.at[step, part],
                dst_ref=halo.at[step, side, part],
                send_sem=halo_send.at[step, side, chunk],
                recv_sem=halo_recv.at[step, side, chunk],
                device_id={"row": target},
                device_id_type=MESH,
            )
            for side, target in ((0, right), (1, left))
        ]

    def keep(slot, first, value):
        h, l = split(value)
        high[slot, pl.ds(first, value.shape[0])] = h
        low[slot, pl.ds(first, value.shape[0])] = l

    for chunk in range(chunks):
        span = per * bs
        piece = vec_ref[:, chunk * span:(chunk + 1) * span]
        turned = piece.T.reshape(per, bs, width)
        fields[0, chunk * per:(chunk + 1) * per] = turned
        if chunk == 0:
            pl.semaphore_wait(barrier, len(greeted))
        for copy in halo_copies(0, chunk):
            copy.start()
        keep(0, br + chunk * per, turned)

    @pl.loop(0, br)
    def _(i):
        h, l = split(blocks_ref[i])
        ablk[i, :bs] = h
        ablk[i, bs:] = l

    for step in range(3):
        slot, later = step % 2, (step + 1) % 2

        @pl.loop(0, chunks)
        def _(chunk):
            for side, copy in enumerate(halo_copies(step, chunk)):
                copy.wait_recv()
                keep(slot, side * 2 * br + chunk * per, halo[step, side, pl.ds(chunk * per, per)])

        @pl.loop(0, chunks)
        def _(chunk):
            @pl.loop(0, per, unroll=2)
            def _(inner):
                i = chunk * per + inner
                found_high, found_low = [], []
                for s in range(slots):
                    c = lax.rem(cols_ref[i, s] - me * br + br + total, total)
                    c = jnp.clip(c, 0, 3 * br - 1)
                    found_high.append(high[slot, c])
                    found_low.append(low[slot, c])
                b_high = jnp.concatenate(found_high, axis=0)
                b_low = jnp.concatenate(found_low, axis=0)
                a = ablk[i]
                if width % 128 == 0:
                    out = jnp.dot(
                        a, jnp.concatenate([b_high, b_low], axis=1), preferred_element_type=F32
                    )
                    p, q = out[:, :width], out[:, width:]
                    result = p[:bs] + (p[bs:] + q[:bs])
                else:
                    p = jnp.dot(a, b_high, preferred_element_type=F32)
                    q = jnp.dot(a[:bs], b_low, preferred_element_type=F32)
                    result = p[:bs] + (p[bs:] + q)
                value = (result - center * fields[step, i]) * inverse
                if step > 0:
                    value = 2.0 * value - fields[step - 1, i]
                fields[step + 1, i] = value
                if step < 2:
                    h, l = split(value)
                    high[later, br + i] = h
                    low[later, br + i] = l

            if step < 2:
                for copy in halo_copies(step + 1, chunk):
                    copy.start()

    share = br // bundles

    def stack_copy(index):
        target = others[index]
        return pltpu.make_async_remote_copy(
            src_ref=fields.at[3, pl.ds(target["bundle"] * share, share)],
            dst_ref=stacked_ref.at[mine],
            send_sem=all_send.at[index],
            recv_sem=all_recv.at[index],
            device_id=target,
            device_id_type=MESH,
        )

    for index in range(bundles - 1):
        stack_copy(index).start()
    stacked_ref[mine] = fields[3, pl.ds(mine * share, share)]
    for index in range(bundles - 1):
        stack_copy(index).wait_recv()

    held = [stacked_ref[b].reshape(share * bs, width) for b in range(bundles)]
    whole = jnp.concatenate(held, axis=1)
    h, l = split(whole)
    over_rows = (((0,), (0,)), ((), ()))
    main = lax.dot_general(h, h, over_rows, preferred_element_type=F32)
    cross = lax.dot_general(h, l, over_rows, preferred_element_type=F32)
    gram_in[0] = main + (cross + cross.T)

    for index, device in enumerate(partners):
        copy = pltpu.make_async_remote_copy(
            src_ref=gram_in.at[2 * index],
            dst_ref=gram_in.at[2 * index + 1],
            send_sem=gram_send.at[index],
            recv_sem=gram_recv.at[index],
            device_id=device,
            device_id_type=MESH,
        )
        copy.start()
        copy.wait_recv()
        gram_in[2 * index + 2] = gram_in[2 * index] + gram_in[2 * index + 1]
        copy.wait_send()
    gram_ref[...] = gram_in[2 * len(partners)]

    for index in range(bundles - 1):
        stack_copy(index).wait_send()

    for step in range(3):
        @pl.loop(0, chunks)
        def _(chunk):
            for copy in halo_copies(step, chunk):
                copy.wait_send()


def triangular_inverse(block):
    size = block.shape[0]
    row = lax.broadcasted_iota(jnp.int32, (size, size), 0)
    col = lax.broadcasted_iota(jnp.int32, (size, size), 1)
    eye = (row == col).astype(F32)
    work = jnp.concatenate([block, eye], axis=1)
    index = lax.broadcasted_iota(jnp.int32, (size, 1), 0)
    scales = jnp.zeros((size, 1), F32)
    for k in range(size):
        pivot = work[k:k + 1, k:k + 1]
        line = work[k:k + 1, :] * (1.0 / pivot)
        factor = jnp.where(index > k, work[:, k:k + 1], 0.0)
        scales = jnp.where(index == k, pivot, scales)
        work = work - factor * line
    return work[:, size:] * lax.rsqrt(scales)


def factor_kernel(gram_ref, stacked_ref, basis_ref, factor_ref, work):
    n = gram_ref.shape[0]
    row = lax.broadcasted_iota(jnp.int32, (n, n), 0)
    col = lax.broadcasted_iota(jnp.int32, (n, n), 1)
    work[:, :n] = gram_ref[...]
    work[:, n:] = (row == col).astype(F32)
    for first in range(0, n, PANEL):
        last = first + PANEL
        inverse = triangular_inverse(work[first:last, first:last])
        lines = jnp.dot(inverse, work[first:last, :], precision=HIGHEST, preferred_element_type=F32)
        work[first:last, :] = lines
        if last < n:
            work[last:, :] = work[last:, :] - lax.dot_general(
                lines[:, last:n], lines, (((0,), (0,)), ((), ())),
                precision=HIGHEST, preferred_element_type=F32,
            )
    factor_ref[...] = jnp.where(col >= row, work[:, :n], 0.0)
    solver = jnp.where(col <= row, work[:, n:], 0.0)
    bundles, share, bs, width = stacked_ref.shape
    h, l = split(solver)
    over_last = (((1,), (1,)), ((), ()))
    held = [stacked_ref[b].reshape(share * bs, width) for b in range(bundles)]
    fh, fl = split(jnp.concatenate(held, axis=1))
    dot = lambda a, b: lax.dot_general(a, b, over_last, preferred_element_type=F32)
    basis_ref[...] = dot(h, fh) + (dot(h, fl) + dot(l, fh))


def solution(mesh):
    rows, bundles = mesh.shape["row"], mesh.shape["bundle"]
    steps = (rows.bit_length() - 1) + (bundles.bit_length() - 1)
    vmem = pl.BlockSpec(memory_space=pltpu.VMEM)
    smem = pl.BlockSpec(memory_space=pltpu.SMEM)

    def local(vectors, blocks, columns, bounds):
        br, bs, wide = blocks.shape
        width = vectors.shape[0]
        count = width * bundles
        share = br // bundles
        stacked, gram = pl.pallas_call(
            functools.partial(filter_kernel, rows, bundles),
            out_shape=(
                jax.ShapeDtypeStruct((bundles, share, bs, width), F32),
                jax.ShapeDtypeStruct((count, count), F32),
            ),
            in_specs=[smem, smem, vmem, vmem],
            out_specs=(vmem, vmem),
            scratch_shapes=[
                pltpu.VMEM((br, 2 * bs, wide), BF16),
                pltpu.VMEM((2, 3 * br, bs, width), BF16),
                pltpu.VMEM((2, 3 * br, bs, width), BF16),
                pltpu.VMEM((4, br, bs, width), F32),
                pltpu.VMEM((3, 2, br, bs, width), F32),
                pltpu.VMEM((2 * steps + 1, count, count), F32),
                pltpu.SemaphoreType.DMA((3, 2, 4)),
                pltpu.SemaphoreType.DMA((3, 2, 4)),
                pltpu.SemaphoreType.DMA((max(bundles - 1, 1),)),
                pltpu.SemaphoreType.DMA((max(bundles - 1, 1),)),
                pltpu.SemaphoreType.DMA((steps,)),
                pltpu.SemaphoreType.DMA((steps,)),
            ],
            compiler_params=pltpu.CompilerParams(
                collective_id=0, has_side_effects=True, vmem_limit_bytes=VMEM_LIMIT
            ),
        )(columns, bounds, vectors, blocks)
        return pl.pallas_call(
            factor_kernel,
            out_shape=(
                jax.ShapeDtypeStruct((count, share * bs), F32),
                jax.ShapeDtypeStruct((count, count), F32),
            ),
            in_specs=[vmem, vmem],
            out_specs=(vmem, vmem),
            scratch_shapes=[pltpu.VMEM((count, 2 * count), F32)],
            compiler_params=pltpu.CompilerParams(vmem_limit_bytes=VMEM_LIMIT),
        )(gram, stacked)

    placed = (P("bundle", "row"), P("row", None, None), P("row", None), P())
    return jax.shard_map(
        local,
        mesh=mesh,
        in_specs=placed,
        out_specs=(P(None, ("row", "bundle")), P()),
        check_vma=False,
    )
```

```python
import functools

import jax
import jax.numpy as jnp
from jax import lax
from jax.experimental import pallas as pl
from jax.experimental.pallas import tpu as pltpu
from jax.sharding import PartitionSpec as P

MESH = pl.DeviceIdType.MESH
F32 = jnp.float32
BF16 = jnp.bfloat16
HIGHEST = lax.Precision.HIGHEST
VMEM_LIMIT = 56 * 1024 * 1024
PANEL = 64
GROUP = 4
OVER_ROWS = (((0,), (0,)), ((), ()))
OVER_LAST = (((1,), (1,)), ((), ()))


def split(value):
    high = value.astype(BF16)
    return high, (value - high.astype(F32)).astype(BF16)


def filter_kernel(
    rows, bundles, out_count, cols_ref, bounds_ref, vec_ref, blocks_ref, *refs,
):
    outs = refs[:out_count]
    (
        ablk, high, low, fields, halo, sums, lines, halo_send, halo_recv, all_send, all_recv,
        sum_send, sum_recv,
    ) = refs[out_count:]
    me = lax.axis_index("row")
    mine = lax.axis_index("bundle")
    br, bs = blocks_ref.shape[0], blocks_ref.shape[1]
    slots = cols_ref.shape[1]
    width = vec_ref.shape[0]
    total = br * rows
    right = lax.rem(me + 1, rows)
    left = lax.rem(me + rows - 1, rows)
    chunks = 4
    per = br // chunks

    row_bits = rows.bit_length() - 1
    bundle_bits = bundles.bit_length() - 1
    partners = []
    for bit in range(row_bits):
        mask = 1 << bit
        upper = lax.rem(lax.div(me, mask), 2)
        partners.append({"row": me + mask - 2 * mask * upper})
    for bit in range(bundle_bits):
        mask = 1 << bit
        upper = lax.rem(lax.div(mine, mask), 2)
        partners.append({"bundle": mine + mask - 2 * mask * upper})
    others = [{"bundle": lax.rem(mine + step, bundles)} for step in range(1, bundles)]

    barrier = pltpu.get_barrier_semaphore()
    greeted = [{"row": left}, {"row": right}] + partners + others
    for device in greeted:
        pl.semaphore_signal(barrier, inc=1, device_id=device, device_id_type=MESH)

    center = (bounds_ref[0] + bounds_ref[1]) * 0.5
    inverse = 1.0 / ((bounds_ref[1] - bounds_ref[0]) * 0.5)

    def halo_copies(step, chunk):
        part = pl.ds(chunk * per, per)
        return [
            pltpu.make_async_remote_copy(
                src_ref=fields.at[step, part],
                dst_ref=halo.at[step, side, part],
                send_sem=halo_send.at[step, side, chunk],
                recv_sem=halo_recv.at[step, side, chunk],
                device_id={"row": target},
                device_id_type=MESH,
            )
            for side, target in ((0, right), (1, left))
        ]

    def keep(slot, first, value):
        h, l = split(value)
        high[slot, pl.ds(first, value.shape[0])] = h
        low[slot, pl.ds(first, value.shape[0])] = l

    for chunk in range(chunks):
        span = per * bs
        piece = vec_ref[:, chunk * span:(chunk + 1) * span]
        turned = piece.T.reshape(per, bs, width)
        fields[0, chunk * per:(chunk + 1) * per] = turned
        if chunk == 0:
            pl.semaphore_wait(barrier, len(greeted))
        for copy in halo_copies(0, chunk):
            copy.start()
        keep(0, br + chunk * per, turned)

    @pl.loop(0, br)
    def _(i):
        h, l = split(blocks_ref[i])
        ablk[i, :bs] = h
        ablk[i, bs:] = l

    def receive(step):
        slot = step % 2

        @pl.loop(0, chunks)
        def _(chunk):
            for side, copy in enumerate(halo_copies(step, chunk)):
                copy.wait_recv()
                keep(slot, side * 2 * br + chunk * per, halo[step, side, pl.ds(chunk * per, per)])

    def apply_chunk(step, chunk):
        slot, later = step % 2, (step + 1) % 2

        @pl.loop(0, per, unroll=2)
        def _(inner):
            i = chunk * per + inner
            found_high, found_low = [], []
            for s in range(slots):
                c = lax.rem(cols_ref[i, s] - me * br + br + total, total)
                c = jnp.clip(c, 0, 3 * br - 1)
                found_high.append(high[slot, c])
                found_low.append(low[slot, c])
            b_high = jnp.concatenate(found_high, axis=0)
            b_low = jnp.concatenate(found_low, axis=0)
            a = ablk[i]
            if width % 128 == 0:
                out = jnp.dot(
                    a, jnp.concatenate([b_high, b_low], axis=1), preferred_element_type=F32
                )
                p, q = out[:, :width], out[:, width:]
                result = p[:bs] + (p[bs:] + q[:bs])
            else:
                p = jnp.dot(a, b_high, preferred_element_type=F32)
                q = jnp.dot(a[:bs], b_low, preferred_element_type=F32)
                result = p[:bs] + (p[bs:] + q)
            value = (result - center * fields[step, i]) * inverse
            if step > 0:
                value = 2.0 * value - fields[step - 1, i]
            fields[step + 1, i] = value
            if step < 2:
                h, l = split(value)
                high[later, br + i] = h
                low[later, br + i] = l

    for step in range(2):
        receive(step)

        @pl.loop(0, chunks)
        def _(chunk):
            apply_chunk(step, chunk)
            for copy in halo_copies(step + 1, chunk):
                copy.start()

    share = br // bundles
    receive(2)

    def sum_copy(index, device):
        return pltpu.make_async_remote_copy(
            src_ref=sums.at[2 * index],
            dst_ref=sums.at[2 * index + 1],
            send_sem=sum_send.at[index],
            recv_sem=sum_recv.at[index],
            device_id=device,
            device_id_type=MESH,
        )

    def sum_step(index, device, beside=None):
        copy = sum_copy(index, device)
        copy.start()
        if beside is not None:
            next(beside, None)
        copy.wait()
        sums[2 * index + 2] = sums[2 * index] + sums[2 * index + 1]

    if is_paired(bundles, width):
        stacked_ref, corner_ref, diag_ref, cross_ref = outs
        theirs = 1 - mine
        half = chunks // 2

        def stack_copy(part):
            rows_of = pl.ds(theirs * share + part * per, per)
            return pltpu.make_async_remote_copy(
                src_ref=fields.at[3, rows_of],
                dst_ref=stacked_ref.at[mine, pl.ds(part * per, per)],
                send_sem=all_send.at[part],
                recv_sem=all_recv.at[part],
                device_id={"bundle": theirs},
                device_id_type=MESH,
            )

        @pl.loop(0, half)
        def _(part):
            apply_chunk(2, theirs * half + part)
            stack_copy(part).start()

        @pl.loop(0, half)
        def _(part):
            apply_chunk(2, mine * half + part)

        stacked_ref[mine] = fields[3, pl.ds(mine * share, share)]
        h, l = split(fields[3].reshape(br * bs, width))
        both = lax.dot_general(
            h, jnp.concatenate([h, l], axis=1), OVER_ROWS, preferred_element_type=F32
        )
        sums[0] = both[:, :width] + (both[:, width:] + both[:, width:].T)
        for index in range(row_bits):
            sum_step(index, partners[index])
        done = 2 * row_bits
        diag_ref[mine] = sums[done]
        diag_copy = pltpu.make_async_remote_copy(
            src_ref=sums.at[done],
            dst_ref=diag_ref.at[mine],
            send_sem=all_send.at[half],
            recv_sem=all_recv.at[half],
            device_id={"bundle": theirs},
            device_id_type=MESH,
        )
        diag_copy.start()
        for part in range(half):
            stack_copy(part).wait_recv()
        h0, l0 = split(stacked_ref[0].reshape(share * bs, width))
        h1, l1 = split(stacked_ref[1].reshape(share * bs, width))
        both = lax.dot_general(
            h0, jnp.concatenate([h1, l1], axis=1), OVER_ROWS, preferred_element_type=F32
        )
        rest = lax.dot_general(l0, h1, OVER_ROWS, preferred_element_type=F32)
        sums[done + 2] = both[:, :width] + (both[:, width:] + rest)
        diag_copy.wait()
        found = []
        pieces = factor_steps(diag_ref[0], lines, found)
        for bit, device in enumerate(partners):
            sum_step(row_bits + 1 + bit, device, pieces)
        for _ in pieces:
            pass
        cross_ref[...] = sums[done + 2 + 2 * len(partners)]
        corner_ref[0], corner_ref[1] = found
        for part in range(half):
            stack_copy(part).wait_send()
    else:
        stacked_ref, gram_ref = outs

        @pl.loop(0, chunks)
        def _(chunk):
            apply_chunk(2, chunk)

        def stack_copy(index):
            target = others[index]
            return pltpu.make_async_remote_copy(
                src_ref=fields.at[3, pl.ds(target["bundle"] * share, share)],
                dst_ref=stacked_ref.at[mine],
                send_sem=all_send.at[index],
                recv_sem=all_recv.at[index],
                device_id=target,
                device_id_type=MESH,
            )

        for index in range(bundles - 1):
            stack_copy(index).start()
        stacked_ref[mine] = fields[3, pl.ds(mine * share, share)]
        for index in range(bundles - 1):
            stack_copy(index).wait_recv()
        held = [stacked_ref[b].reshape(share * bs, width) for b in range(bundles)]
        h, l = split(jnp.concatenate(held, axis=1))
        main = lax.dot_general(h, h, OVER_ROWS, preferred_element_type=F32)
        cross = lax.dot_general(h, l, OVER_ROWS, preferred_element_type=F32)
        sums[0] = main + (cross + cross.T)
        for index, device in enumerate(partners):
            sum_step(index, device)
        gram_ref[...] = sums[2 * len(partners)]
        for index in range(bundles - 1):
            stack_copy(index).wait_send()

    for step in range(3):
        @pl.loop(0, chunks)
        def _(chunk):
            for copy in halo_copies(step, chunk):
                copy.wait_send()


def is_paired(bundles, width):
    return bundles == 2 and width % 128 == 0


def dot(a, b, dims=(((1,), (0,)), ((), ()))):
    return lax.dot_general(a, b, dims, precision=HIGHEST, preferred_element_type=F32)


def upper_part(value, lower=False):
    row = lax.broadcasted_iota(jnp.int32, value.shape, 0)
    col = lax.broadcasted_iota(jnp.int32, value.shape, 1)
    return jnp.where((col <= row) if lower else (col >= row), value, 0.0)


def factor_steps(block, lines, found):
    size = block.shape[0]
    if size > PANEL:
        half = size // 2
        part = []
        yield from factor_steps(block[:half, :half], lines, part)
        upper0, inverse0 = part
        corner = dot(inverse0, block[:half, half:])
        rest = block[half:, half:] - dot(corner, corner, OVER_ROWS)
        part = []
        yield from factor_steps(rest, lines, part)
        upper1, inverse1 = part
        side = -dot(inverse1, dot(corner, inverse0, OVER_ROWS))
        zero = jnp.zeros((half, size - half), F32)
        found.append(
            jnp.concatenate(
                [
                    jnp.concatenate([upper0, corner], axis=1),
                    jnp.concatenate([zero.T, upper1], axis=1),
                ],
                axis=0,
            )
        )
        found.append(
            jnp.concatenate(
                [
                    jnp.concatenate([inverse0, zero], axis=1),
                    jnp.concatenate([side, inverse1], axis=1),
                ],
                axis=0,
            )
        )
        return
    row = lax.broadcasted_iota(jnp.int32, (size, size), 0)
    col = lax.broadcasted_iota(jnp.int32, (size, size), 1)
    work = jnp.concatenate([block, (row == col).astype(F32)], axis=1)
    for first in range(0, size, GROUP):
        top = first // 8 * 8
        if first and first % 8 == 0:
            work = work[8:]
        index = lax.broadcasted_iota(jnp.int32, work.shape, 0)
        columns = [
            jnp.broadcast_to(work[:, first + j:first + j + 1], work.shape) for j in range(GROUP)
        ]
        for j in range(GROUP):
            at = first + j - top
            pivot = columns[j][at:at + 1]
            turned = 1.0 / pivot
            line = work[at:at + 1]
            lines[first + j:first + j + 1] = line * lax.rsqrt(pivot)
            factor = jnp.where(index > at, columns[j], 0.0)
            for m in range(j + 1, GROUP):
                columns[m] = columns[m] - factor * (columns[m][at:at + 1] * turned)
            work = work - factor * (line * turned)
        if (first + GROUP) % 32 == 0 and first + GROUP < size:
            yield
    found.append(upper_part(lines[:, :size]))
    found.append(upper_part(lines[:, size:], lower=True))
    yield


def write_basis(solver, fields, basis_ref, first):
    h, l = split(solver)
    fh, fl = split(fields)
    product = lambda a, b: lax.dot_general(a, b, OVER_LAST, preferred_element_type=F32)
    basis_ref[first:first + solver.shape[0]] = product(h, fh) + (product(h, fl) + product(l, fh))


def factor_kernel(gram_ref, stacked_ref, basis_ref, factor_ref, lines):
    found = []
    for _ in factor_steps(gram_ref[...], lines, found):
        pass
    factor_ref[...] = found[0]
    bundles, share, bs, width = stacked_ref.shape
    held = [stacked_ref[b].reshape(share * bs, width) for b in range(bundles)]
    write_basis(found[1], jnp.concatenate(held, axis=1), basis_ref, 0)


def finish_kernel(corner_ref, diag_ref, cross_ref, stacked_ref, basis_ref, factor_ref, lines):
    bundles, share, bs, width = stacked_ref.shape
    upper0, inverse0 = corner_ref[0], corner_ref[1]
    field0 = stacked_ref[0].reshape(share * bs, width)
    field1 = stacked_ref[1].reshape(share * bs, width)
    corner = dot(inverse0, cross_ref[...])
    rest = diag_ref[1] - dot(corner, corner, OVER_ROWS)
    side = dot(corner, inverse0, OVER_ROWS)
    factor_ref[:width, :width] = upper0
    factor_ref[:width, width:] = corner
    factor_ref[width:, :width] = jnp.zeros((width, width), F32)
    write_basis(inverse0, field0, basis_ref, 0)
    found = []
    for _ in factor_steps(rest, lines, found):
        pass
    upper1, inverse1 = found
    factor_ref[width:, width:] = upper1
    solver = jnp.concatenate([-dot(inverse1, side), inverse1], axis=1)
    write_basis(solver, jnp.concatenate([field0, field1], axis=1), basis_ref, width)


def solution(mesh):
    rows, bundles = mesh.shape["row"], mesh.shape["bundle"]
    row_bits, bundle_bits = rows.bit_length() - 1, bundles.bit_length() - 1
    vmem = pl.BlockSpec(memory_space=pltpu.VMEM)
    smem = pl.BlockSpec(memory_space=pltpu.SMEM)

    def local(vectors, blocks, columns, bounds):
        br, bs, wide = blocks.shape
        width = vectors.shape[0]
        count = width * bundles
        share = br // bundles
        paired = is_paired(bundles, width)
        panel = min(PANEL, width) if paired else min(PANEL, count)
        block = jax.ShapeDtypeStruct((width, width), F32)
        two = jax.ShapeDtypeStruct((2, width, width), F32)
        stack = jax.ShapeDtypeStruct((bundles, share, bs, width), F32)
        if paired:
            shapes = (stack, two, two, block)
            side, sums, copies = width, 2 * row_bits + bundle_bits + 1, 3
        else:
            shapes = (stack, jax.ShapeDtypeStruct((count, count), F32))
            side, sums, copies = count, row_bits + bundle_bits, max(bundles - 1, 1)
        parts = pl.pallas_call(
            functools.partial(filter_kernel, rows, bundles, len(shapes)),
            out_shape=shapes,
            in_specs=[smem, smem, vmem, vmem],
            out_specs=tuple(vmem for _ in shapes),
            scratch_shapes=[
                pltpu.VMEM((br, 2 * bs, wide), BF16),
                pltpu.VMEM((2, 3 * br, bs, width), BF16),
                pltpu.VMEM((2, 3 * br, bs, width), BF16),
                pltpu.VMEM((4, br, bs, width), F32),
                pltpu.VMEM((3, 2, br, bs, width), F32),
                pltpu.VMEM((2 * sums + 1, side, side), F32),
                pltpu.VMEM((panel, 2 * panel), F32),
                pltpu.SemaphoreType.DMA((3, 2, 4)),
                pltpu.SemaphoreType.DMA((3, 2, 4)),
                pltpu.SemaphoreType.DMA((copies,)),
                pltpu.SemaphoreType.DMA((copies,)),
                pltpu.SemaphoreType.DMA((sums,)),
                pltpu.SemaphoreType.DMA((sums,)),
            ],
            compiler_params=pltpu.CompilerParams(
                collective_id=0, has_side_effects=True, vmem_limit_bytes=VMEM_LIMIT
            ),
        )(columns, bounds, vectors, blocks)
        operands = parts[1:] + parts[:1]
        return pl.pallas_call(
            finish_kernel if paired else factor_kernel,
            out_shape=(
                jax.ShapeDtypeStruct((count, share * bs), F32),
                jax.ShapeDtypeStruct((count, count), F32),
            ),
            in_specs=[vmem] * len(operands),
            out_specs=(vmem, vmem),
            scratch_shapes=[pltpu.VMEM((panel, 2 * panel), F32)],
            compiler_params=pltpu.CompilerParams(vmem_limit_bytes=VMEM_LIMIT),
        )(*operands)

    placed = (P("bundle", "row"), P("row", None, None), P("row", None), P())
    return jax.shard_map(
        local,
        mesh=mesh,
        in_specs=placed,
        out_specs=(P(None, ("row", "bundle")), P()),
        check_vma=False,
    )
```

```python
import functools

import jax
import jax.numpy as jnp
from jax import lax
from jax.experimental import pallas as pl
from jax.experimental.pallas import tpu as pltpu
from jax.sharding import PartitionSpec as P

MESH = pl.DeviceIdType.MESH
F32 = jnp.float32
BF16 = jnp.bfloat16
HIGHEST = lax.Precision.HIGHEST
VMEM_LIMIT = 56 * 1024 * 1024
PANEL = 64
GROUP = 4
CHUNKS = 4
OVER_ROWS = (((0,), (0,)), ((), ()))
OVER_LAST = (((1,), (1,)), ((), ()))


def split(value):
    high = value.astype(BF16)
    return high, (value - high.astype(F32)).astype(BF16)


def filter_kernel(
    rows, bundles, cols_ref, bounds_ref, vec_ref, blocks_ref, stacked_ref, gram_ref,
    ablk, high, low, fields, halo, sums, halo_send, halo_recv, all_send, all_recv,
    sum_send, sum_recv,
):
    me = lax.axis_index("row")
    mine = lax.axis_index("bundle")
    br, bs = blocks_ref.shape[0], blocks_ref.shape[1]
    slots = cols_ref.shape[1]
    width = vec_ref.shape[0]
    total = br * rows
    right = lax.rem(me + 1, rows)
    left = lax.rem(me + rows - 1, rows)
    chunks = 4
    per = br // chunks

    row_bits = rows.bit_length() - 1
    bundle_bits = bundles.bit_length() - 1
    partners = []
    for bit in range(row_bits):
        mask = 1 << bit
        upper = lax.rem(lax.div(me, mask), 2)
        partners.append({"row": me + mask - 2 * mask * upper})
    for bit in range(bundle_bits):
        mask = 1 << bit
        upper = lax.rem(lax.div(mine, mask), 2)
        partners.append({"bundle": mine + mask - 2 * mask * upper})
    others = [{"bundle": lax.rem(mine + step, bundles)} for step in range(1, bundles)]

    barrier = pltpu.get_barrier_semaphore()
    greeted = [{"row": left}, {"row": right}] + partners + others
    for device in greeted:
        pl.semaphore_signal(barrier, inc=1, device_id=device, device_id_type=MESH)

    center = (bounds_ref[0] + bounds_ref[1]) * 0.5
    inverse = 1.0 / ((bounds_ref[1] - bounds_ref[0]) * 0.5)

    def halo_copies(step, chunk):
        part = pl.ds(chunk * per, per)
        return [
            pltpu.make_async_remote_copy(
                src_ref=fields.at[step, part],
                dst_ref=halo.at[step, side, part],
                send_sem=halo_send.at[step, side, chunk],
                recv_sem=halo_recv.at[step, side, chunk],
                device_id={"row": target},
                device_id_type=MESH,
            )
            for side, target in ((0, right), (1, left))
        ]

    def keep(slot, first, value):
        h, l = split(value)
        high[slot, pl.ds(first, value.shape[0])] = h
        low[slot, pl.ds(first, value.shape[0])] = l

    for chunk in range(chunks):
        span = per * bs
        piece = vec_ref[:, chunk * span:(chunk + 1) * span]
        turned = piece.T.reshape(per, bs, width)
        fields[0, chunk * per:(chunk + 1) * per] = turned
        if chunk == 0:
            pl.semaphore_wait(barrier, len(greeted))
        for copy in halo_copies(0, chunk):
            copy.start()
        keep(0, br + chunk * per, turned)

    @pl.loop(0, br)
    def _(i):
        h, l = split(blocks_ref[i])
        ablk[i, :bs] = h
        ablk[i, bs:] = l

    def receive(step):
        slot = step % 2

        @pl.loop(0, chunks)
        def _(chunk):
            for side, copy in enumerate(halo_copies(step, chunk)):
                copy.wait_recv()
                keep(slot, side * 2 * br + chunk * per, halo[step, side, pl.ds(chunk * per, per)])

    def apply_chunk(step, chunk):
        slot, later = step % 2, (step + 1) % 2

        @pl.loop(0, per, unroll=2)
        def _(inner):
            i = chunk * per + inner
            found_high, found_low = [], []
            for s in range(slots):
                c = lax.rem(cols_ref[i, s] - me * br + br + total, total)
                c = jnp.clip(c, 0, 3 * br - 1)
                found_high.append(high[slot, c])
                found_low.append(low[slot, c])
            b_high = jnp.concatenate(found_high, axis=0)
            b_low = jnp.concatenate(found_low, axis=0)
            a = ablk[i]
            if width % 128 == 0:
                out = jnp.dot(
                    a, jnp.concatenate([b_high, b_low], axis=1), preferred_element_type=F32
                )
                p, q = out[:, :width], out[:, width:]
                result = p[:bs] + (p[bs:] + q[:bs])
            else:
                p = jnp.dot(a, b_high, preferred_element_type=F32)
                q = jnp.dot(a[:bs], b_low, preferred_element_type=F32)
                result = p[:bs] + (p[bs:] + q)
            value = (result - center * fields[step, i]) * inverse
            if step > 0:
                value = 2.0 * value - fields[step - 1, i]
            fields[step + 1, i] = value
            if step < 2:
                h, l = split(value)
                high[later, br + i] = h
                low[later, br + i] = l

    for step in range(2):
        receive(step)

        @pl.loop(0, chunks)
        def _(chunk):
            apply_chunk(step, chunk)
            for copy in halo_copies(step + 1, chunk):
                copy.start()

    share = br // bundles
    receive(2)

    def sum_copy(index, device):
        return pltpu.make_async_remote_copy(
            src_ref=sums.at[2 * index],
            dst_ref=sums.at[2 * index + 1],
            send_sem=sum_send.at[index],
            recv_sem=sum_recv.at[index],
            device_id=device,
            device_id_type=MESH,
        )

    def sum_step(index, device):
        copy = sum_copy(index, device)
        copy.start()
        copy.wait()
        sums[2 * index + 2] = sums[2 * index] + sums[2 * index + 1]

    @pl.loop(0, chunks)
    def _(chunk):
        apply_chunk(2, chunk)

    def stack_copy(index):
        target = others[index]
        return pltpu.make_async_remote_copy(
            src_ref=fields.at[3, pl.ds(target["bundle"] * share, share)],
            dst_ref=stacked_ref.at[mine],
            send_sem=all_send.at[index],
            recv_sem=all_recv.at[index],
            device_id=target,
            device_id_type=MESH,
        )

    for index in range(bundles - 1):
        stack_copy(index).start()
    stacked_ref[mine] = fields[3, pl.ds(mine * share, share)]
    for index in range(bundles - 1):
        stack_copy(index).wait_recv()
    held = [stacked_ref[b].reshape(share * bs, width) for b in range(bundles)]
    h, l = split(jnp.concatenate(held, axis=1))
    main = lax.dot_general(h, h, OVER_ROWS, preferred_element_type=F32)
    cross = lax.dot_general(h, l, OVER_ROWS, preferred_element_type=F32)
    sums[0] = main + (cross + cross.T)
    for index, device in enumerate(partners):
        sum_step(index, device)
    gram_ref[...] = sums[2 * len(partners)]
    for index in range(bundles - 1):
        stack_copy(index).wait_send()

    for step in range(3):
        @pl.loop(0, chunks)
        def _(chunk):
            for copy in halo_copies(step, chunk):
                copy.wait_send()


def paired_kernel(
    rows, cols_ref, bounds_ref, vec_ref, blocks_ref, stacked_ref, corner_ref, diag_ref, cross_ref,
    ablk, picks, fields, halo, whole, arrived, sums, lines, halo_send, halo_recv, all_send,
    all_recv, sum_send, sum_recv,
):
    me = lax.axis_index("row")
    mine = lax.axis_index("bundle")
    theirs = 1 - mine
    br, bs = blocks_ref.shape[0], blocks_ref.shape[1]
    slots = cols_ref.shape[1]
    width = vec_ref.shape[0]
    part = width // 2
    total = br * rows
    pairs = br // 2
    chunks = CHUNKS
    per = pairs // chunks
    right = lax.rem(me + 1, rows)
    left = lax.rem(me + rows - 1, rows)
    row_bits = rows.bit_length() - 1
    partners = []
    for bit in range(row_bits):
        mask = 1 << bit
        upper = lax.rem(lax.div(me, mask), 2)
        partners.append({"row": me + mask - 2 * mask * upper})
    partners.append({"bundle": theirs})

    barrier = pltpu.get_barrier_semaphore()
    greeted = [{"row": left}, {"row": right}] + partners
    for device in greeted:
        pl.semaphore_signal(barrier, inc=1, device_id=device, device_id_type=MESH)

    center = (bounds_ref[0] + bounds_ref[1]) * 0.5
    inverse = 1.0 / ((bounds_ref[1] - bounds_ref[0]) * 0.5)
    in_low = lax.broadcasted_iota(jnp.int32, (bs, width), 1) < part
    turn = lambda value: pltpu.roll(value, part, 1)

    def halo_copies(step, half, chunk):
        span = pl.ds(chunk * per, per)
        return [
            pltpu.make_async_remote_copy(
                src_ref=fields.at[half, step, span],
                dst_ref=halo.at[step, half, side, span],
                send_sem=halo_send.at[step, half, side, chunk],
                recv_sem=halo_recv.at[step, half, side, chunk],
                device_id={"row": target},
                device_id_type=MESH,
            )
            for side, target in ((0, right), (1, left))
        ]

    def keep(half, pair, value):
        h = value.astype(BF16).astype(F32)
        l = value - h
        picks[half, 2 * pair] = jnp.where(in_low, h, turn(l)).astype(BF16)
        picks[half, 2 * pair + 1] = jnp.where(in_low, turn(h), l).astype(BF16)

    def unpack(even_half, odd_half):
        return (
            jnp.where(in_low, even_half, turn(odd_half)),
            jnp.where(in_low, turn(even_half), odd_half),
        )

    for pair in range(pairs):
        turned = vec_ref[:, pair * 2 * bs:(pair + 1) * 2 * bs].T
        fields[0, 0, pair], fields[1, 0, pair] = unpack(turned[:bs], turned[bs:])
        if pair == per - 1:
            pl.semaphore_wait(barrier, len(greeted))
        if (pair + 1) % per == 0:
            for copy in halo_copies(0, 0, pair // per):
                copy.start()

    @pl.loop(0, chunks)
    def _(chunk):
        for copy in halo_copies(0, 1, chunk):
            copy.start()

    @pl.loop(0, br)
    def _(i):
        h, l = split(blocks_ref[i])
        ablk[i, :bs] = h
        ablk[i, bs:] = l

    def receive(step, half):
        @pl.loop(0, pairs, unroll=2)
        def _(pair):
            keep(half, pairs + pair, fields[half, step, pair])

        @pl.loop(0, chunks)
        def _(chunk):
            for side, copy in enumerate(halo_copies(step, half, chunk)):
                copy.wait_recv()
                for inner in range(per):
                    pair = chunk * per + inner
                    keep(half, side * 2 * pairs + pair, halo[step, half, side, pair])

    def apply_chunk(step, half, chunk):
        @pl.loop(0, per, unroll=per)
        def _(inner):
            pair = chunk * per + inner
            results = []
            for odd in range(2):
                i = 2 * pair + odd
                found = []
                for s in range(slots):
                    c = cols_ref[i, s] - me * br + br
                    c = jnp.where(c < 0, c + total, c)
                    c = jnp.where(c >= total, c - total, c)
                    found.append(picks[half, jnp.clip(c, 0, 3 * br - 1)])
                out = jnp.dot(ablk[i], jnp.concatenate(found, axis=0), preferred_element_type=F32)
                result = out[:bs] + out[bs:]
                results.append(result + turn(result))
            result = jnp.where(in_low, results[0], results[1])
            value = (result - center * fields[half, step, pair]) * inverse
            if step > 0:
                value = 2.0 * value - fields[half, step - 1, pair]
            fields[half, step + 1, pair] = value

    for step in range(2):
        for half in range(2):
            receive(step, half)

            @pl.loop(0, chunks)
            def _(chunk):
                apply_chunk(step, half, chunk)
                for copy in halo_copies(step + 1, half, chunk):
                    copy.start()

    share = pairs // 2
    parts = chunks // 2

    def stack_copy(half, index):
        return pltpu.make_async_remote_copy(
            src_ref=fields.at[half, 3, pl.ds(theirs * share + index * per, per)],
            dst_ref=arrived.at[half, pl.ds(index * per, per)],
            send_sem=all_send.at[half, index],
            recv_sem=all_recv.at[half, index],
            device_id={"bundle": theirs},
            device_id_type=MESH,
        )

    for half in range(2):
        receive(2, half)

        @pl.loop(0, parts)
        def _(index):
            apply_chunk(2, half, theirs * parts + index)
            stack_copy(half, index).start()

        @pl.loop(0, parts)
        def _(index):
            apply_chunk(2, half, mine * parts + index)

    @pl.loop(0, pairs, unroll=2)
    def _(pair):
        whole[2 * pair], whole[2 * pair + 1] = unpack(fields[0, 3, pair], fields[1, 3, pair])

    stacked_ref[mine] = whole[pl.ds(mine * 2 * share, 2 * share)]
    h, l = split(whole[...].reshape(br * bs, width))
    both = lax.dot_general(
        h, jnp.concatenate([h, l], axis=1), OVER_ROWS, preferred_element_type=F32
    )
    sums[0] = both[:, :width] + (both[:, width:] + both[:, width:].T)

    def sum_step(index, device, beside=None):
        copy = pltpu.make_async_remote_copy(
            src_ref=sums.at[2 * index],
            dst_ref=sums.at[2 * index + 1],
            send_sem=sum_send.at[index],
            recv_sem=sum_recv.at[index],
            device_id=device,
            device_id_type=MESH,
        )
        copy.start()
        if beside is not None:
            next(beside, None)
        copy.wait()
        sums[2 * index + 2] = sums[2 * index] + sums[2 * index + 1]

    for index in range(row_bits):
        sum_step(index, partners[index])
    done = 2 * row_bits
    diag_ref[mine] = sums[done]
    diag_copy = pltpu.make_async_remote_copy(
        src_ref=sums.at[done],
        dst_ref=diag_ref.at[mine],
        send_sem=sum_send.at[row_bits],
        recv_sem=sum_recv.at[row_bits],
        device_id={"bundle": theirs},
        device_id_type=MESH,
    )
    diag_copy.start()
    for half in range(2):
        for index in range(parts):
            stack_copy(half, index).wait_recv()

    @pl.loop(0, share, unroll=2)
    def _(pair):
        even, odd = unpack(arrived[0, pair], arrived[1, pair])
        stacked_ref[theirs, 2 * pair] = even
        stacked_ref[theirs, 2 * pair + 1] = odd

    h0, l0 = split(stacked_ref[0].reshape(2 * share * bs, width))
    h1, l1 = split(stacked_ref[1].reshape(2 * share * bs, width))
    both = lax.dot_general(
        h0, jnp.concatenate([h1, l1], axis=1), OVER_ROWS, preferred_element_type=F32
    )
    rest = lax.dot_general(l0, h1, OVER_ROWS, preferred_element_type=F32)
    sums[done + 2] = both[:, :width] + (both[:, width:] + rest)
    diag_copy.wait()
    found = []
    pieces = factor_steps(diag_ref[0], lines, found)
    for bit, device in enumerate(partners):
        sum_step(row_bits + 1 + bit, device, pieces)
    for _ in pieces:
        pass
    cross_ref[...] = sums[done + 2 + 2 * len(partners)]
    corner_ref[0], corner_ref[1] = found

    for half in range(2):
        for index in range(parts):
            stack_copy(half, index).wait_send()
        for step in range(3):
            @pl.loop(0, chunks)
            def _(chunk):
                for copy in halo_copies(step, half, chunk):
                    copy.wait_send()


def is_paired(bundles, width):
    return bundles == 2 and width == 128


def dot(a, b, dims=(((1,), (0,)), ((), ()))):
    return lax.dot_general(a, b, dims, precision=HIGHEST, preferred_element_type=F32)


def upper_part(value, lower=False):
    row = lax.broadcasted_iota(jnp.int32, value.shape, 0)
    col = lax.broadcasted_iota(jnp.int32, value.shape, 1)
    return jnp.where((col <= row) if lower else (col >= row), value, 0.0)


def factor_steps(block, lines, found):
    size = block.shape[0]
    if size > PANEL:
        half = size // 2
        part = []
        yield from factor_steps(block[:half, :half], lines, part)
        upper0, inverse0 = part
        corner = dot(inverse0, block[:half, half:])
        rest = block[half:, half:] - dot(corner, corner, OVER_ROWS)
        part = []
        yield from factor_steps(rest, lines, part)
        upper1, inverse1 = part
        side = -dot(inverse1, dot(corner, inverse0, OVER_ROWS))
        zero = jnp.zeros((half, size - half), F32)
        found.append(
            jnp.concatenate(
                [
                    jnp.concatenate([upper0, corner], axis=1),
                    jnp.concatenate([zero.T, upper1], axis=1),
                ],
                axis=0,
            )
        )
        found.append(
            jnp.concatenate(
                [
                    jnp.concatenate([inverse0, zero], axis=1),
                    jnp.concatenate([side, inverse1], axis=1),
                ],
                axis=0,
            )
        )
        return
    row = lax.broadcasted_iota(jnp.int32, (size, size), 0)
    col = lax.broadcasted_iota(jnp.int32, (size, size), 1)
    work = jnp.concatenate([block, (row == col).astype(F32)], axis=1)
    for first in range(0, size, GROUP):
        top = first // 8 * 8
        if first and first % 8 == 0:
            work = work[8:]
        index = lax.broadcasted_iota(jnp.int32, work.shape, 0)
        columns = [
            jnp.broadcast_to(work[:, first + j:first + j + 1], work.shape) for j in range(GROUP)
        ]
        for j in range(GROUP):
            at = first + j - top
            pivot = columns[j][at:at + 1]
            turned = 1.0 / pivot
            line = work[at:at + 1]
            lines[first + j:first + j + 1] = line * lax.rsqrt(pivot)
            factor = jnp.where(index > at, columns[j], 0.0)
            for m in range(j + 1, GROUP):
                columns[m] = columns[m] - factor * (columns[m][at:at + 1] * turned)
            work = work - factor * (line * turned)
        if (first + GROUP) % 32 == 0 and first + GROUP < size:
            yield
    found.append(upper_part(lines[:, :size]))
    found.append(upper_part(lines[:, size:], lower=True))
    yield


def write_basis(solver, fields, basis_ref, first):
    h, l = split(solver)
    fh, fl = split(fields)
    product = lambda a, b: lax.dot_general(a, b, OVER_LAST, preferred_element_type=F32)
    basis_ref[first:first + solver.shape[0]] = product(h, fh) + (product(h, fl) + product(l, fh))


def factor_kernel(gram_ref, stacked_ref, basis_ref, factor_ref, lines):
    found = []
    for _ in factor_steps(gram_ref[...], lines, found):
        pass
    factor_ref[...] = found[0]
    bundles, share, bs, width = stacked_ref.shape
    held = [stacked_ref[b].reshape(share * bs, width) for b in range(bundles)]
    write_basis(found[1], jnp.concatenate(held, axis=1), basis_ref, 0)


def finish_kernel(corner_ref, diag_ref, cross_ref, stacked_ref, basis_ref, factor_ref, lines):
    bundles, share, bs, width = stacked_ref.shape
    upper0, inverse0 = corner_ref[0], corner_ref[1]
    field0 = stacked_ref[0].reshape(share * bs, width)
    field1 = stacked_ref[1].reshape(share * bs, width)
    corner = dot(inverse0, cross_ref[...])
    rest = diag_ref[1] - dot(corner, corner, OVER_ROWS)
    side = dot(corner, inverse0, OVER_ROWS)
    factor_ref[:width, :width] = upper0
    factor_ref[:width, width:] = corner
    factor_ref[width:, :width] = jnp.zeros((width, width), F32)
    write_basis(inverse0, field0, basis_ref, 0)
    found = []
    for _ in factor_steps(rest, lines, found):
        pass
    upper1, inverse1 = found
    factor_ref[width:, width:] = upper1
    solver = jnp.concatenate([-dot(inverse1, side), inverse1], axis=1)
    write_basis(solver, jnp.concatenate([field0, field1], axis=1), basis_ref, width)


def solution(mesh):
    rows, bundles = mesh.shape["row"], mesh.shape["bundle"]
    row_bits, bundle_bits = rows.bit_length() - 1, bundles.bit_length() - 1
    vmem = pl.BlockSpec(memory_space=pltpu.VMEM)
    smem = pl.BlockSpec(memory_space=pltpu.SMEM)

    def local(vectors, blocks, columns, bounds):
        br, bs, wide = blocks.shape
        width = vectors.shape[0]
        count = width * bundles
        share = br // bundles
        paired = is_paired(bundles, width)
        panel = min(PANEL, width) if paired else min(PANEL, count)
        block = jax.ShapeDtypeStruct((width, width), F32)
        two = jax.ShapeDtypeStruct((2, width, width), F32)
        stack = jax.ShapeDtypeStruct((bundles, share, bs, width), F32)
        dma = pltpu.SemaphoreType.DMA
        if paired:
            sums = 2 * row_bits + 2
            kernel = functools.partial(paired_kernel, rows)
            shapes = (stack, two, two, block)
            scratch = [
                pltpu.VMEM((br, 2 * bs, wide), BF16),
                pltpu.VMEM((2, 3 * br, bs, width), BF16),
                pltpu.VMEM((2, 4, br // 2, bs, width), F32),
                pltpu.VMEM((3, 2, 2, br // 2, bs, width), F32),
                pltpu.VMEM((br, bs, width), F32),
                pltpu.VMEM((2, br // 4, bs, width), F32),
                pltpu.VMEM((2 * sums + 1, width, width), F32),
                pltpu.VMEM((panel, 2 * panel), F32),
                dma((3, 2, 2, CHUNKS)),
                dma((3, 2, 2, CHUNKS)),
                dma((2, CHUNKS // 2)),
                dma((2, CHUNKS // 2)),
                dma((sums,)),
                dma((sums,)),
            ]
        else:
            sums = row_bits + bundle_bits
            kernel = functools.partial(filter_kernel, rows, bundles)
            shapes = (stack, jax.ShapeDtypeStruct((count, count), F32))
            scratch = [
                pltpu.VMEM((br, 2 * bs, wide), BF16),
                pltpu.VMEM((2, 3 * br, bs, width), BF16),
                pltpu.VMEM((2, 3 * br, bs, width), BF16),
                pltpu.VMEM((4, br, bs, width), F32),
                pltpu.VMEM((3, 2, br, bs, width), F32),
                pltpu.VMEM((2 * sums + 1, count, count), F32),
                dma((3, 2, 4)),
                dma((3, 2, 4)),
                dma((max(bundles - 1, 1),)),
                dma((max(bundles - 1, 1),)),
                dma((sums,)),
                dma((sums,)),
            ]
        parts = pl.pallas_call(
            kernel,
            out_shape=shapes,
            in_specs=[smem, smem, vmem, vmem],
            out_specs=tuple(vmem for _ in shapes),
            scratch_shapes=scratch,
            compiler_params=pltpu.CompilerParams(
                collective_id=0, has_side_effects=True, vmem_limit_bytes=VMEM_LIMIT
            ),
        )(columns, bounds, vectors, blocks)
        operands = parts[1:] + parts[:1]
        return pl.pallas_call(
            finish_kernel if paired else factor_kernel,
            out_shape=(
                jax.ShapeDtypeStruct((count, share * bs), F32),
                jax.ShapeDtypeStruct((count, count), F32),
            ),
            in_specs=[vmem] * len(operands),
            out_specs=(vmem, vmem),
            scratch_shapes=[pltpu.VMEM((panel, 2 * panel), F32)],
            compiler_params=pltpu.CompilerParams(vmem_limit_bytes=VMEM_LIMIT),
        )(*operands)

    placed = (P("bundle", "row"), P("row", None, None), P("row", None), P())
    return jax.shard_map(
        local,
        mesh=mesh,
        in_specs=placed,
        out_specs=(P(None, ("row", "bundle")), P()),
        check_vma=False,
    )
```

```python
import functools

import jax
import jax.numpy as jnp
from jax import lax
from jax.experimental import pallas as pl
from jax.experimental.pallas import tpu as pltpu
from jax.sharding import PartitionSpec as P

MESH = pl.DeviceIdType.MESH
F32 = jnp.float32
BF16 = jnp.bfloat16
HIGHEST = lax.Precision.HIGHEST
VMEM_LIMIT = 56 * 1024 * 1024
PANEL = 64
GROUP = 8
CHUNKS = 4
OVER_ROWS = (((0,), (0,)), ((), ()))
OVER_LAST = (((1,), (1,)), ((), ()))


def split(value):
    high = value.astype(BF16)
    return high, (value - high.astype(F32)).astype(BF16)


def filter_kernel(
    rows, bundles, cols_ref, bounds_ref, vec_ref, blocks_ref, stacked_ref, gram_ref,
    ablk, high, low, fields, halo, sums, halo_send, halo_recv, all_send, all_recv,
    sum_send, sum_recv,
):
    me = lax.axis_index("row")
    mine = lax.axis_index("bundle")
    br, bs = blocks_ref.shape[0], blocks_ref.shape[1]
    slots = cols_ref.shape[1]
    width = vec_ref.shape[0]
    total = br * rows
    right = lax.rem(me + 1, rows)
    left = lax.rem(me + rows - 1, rows)
    chunks = 4
    per = br // chunks

    row_bits = rows.bit_length() - 1
    bundle_bits = bundles.bit_length() - 1
    partners = []
    for bit in range(row_bits):
        mask = 1 << bit
        upper = lax.rem(lax.div(me, mask), 2)
        partners.append({"row": me + mask - 2 * mask * upper})
    for bit in range(bundle_bits):
        mask = 1 << bit
        upper = lax.rem(lax.div(mine, mask), 2)
        partners.append({"bundle": mine + mask - 2 * mask * upper})
    others = [{"bundle": lax.rem(mine + step, bundles)} for step in range(1, bundles)]

    barrier = pltpu.get_barrier_semaphore()
    greeted = [{"row": left}, {"row": right}] + partners + others
    for device in greeted:
        pl.semaphore_signal(barrier, inc=1, device_id=device, device_id_type=MESH)

    center = (bounds_ref[0] + bounds_ref[1]) * 0.5
    inverse = 1.0 / ((bounds_ref[1] - bounds_ref[0]) * 0.5)

    def halo_copies(step, chunk):
        part = pl.ds(chunk * per, per)
        return [
            pltpu.make_async_remote_copy(
                src_ref=fields.at[step, part],
                dst_ref=halo.at[step, side, part],
                send_sem=halo_send.at[step, side, chunk],
                recv_sem=halo_recv.at[step, side, chunk],
                device_id={"row": target},
                device_id_type=MESH,
            )
            for side, target in ((0, right), (1, left))
        ]

    def keep(slot, first, value):
        h, l = split(value)
        high[slot, pl.ds(first, value.shape[0])] = h
        low[slot, pl.ds(first, value.shape[0])] = l

    for chunk in range(chunks):
        span = per * bs
        piece = vec_ref[:, chunk * span:(chunk + 1) * span]
        turned = piece.T.reshape(per, bs, width)
        fields[0, chunk * per:(chunk + 1) * per] = turned
        if chunk == 0:
            pl.semaphore_wait(barrier, len(greeted))
        for copy in halo_copies(0, chunk):
            copy.start()
        keep(0, br + chunk * per, turned)

    @pl.loop(0, br)
    def _(i):
        h, l = split(blocks_ref[i])
        ablk[i, :bs] = h
        ablk[i, bs:] = l

    def receive(step):
        slot = step % 2

        @pl.loop(0, chunks)
        def _(chunk):
            for side, copy in enumerate(halo_copies(step, chunk)):
                copy.wait_recv()
                keep(slot, side * 2 * br + chunk * per, halo[step, side, pl.ds(chunk * per, per)])

    def apply_chunk(step, chunk):
        slot, later = step % 2, (step + 1) % 2

        @pl.loop(0, per, unroll=2)
        def _(inner):
            i = chunk * per + inner
            found_high, found_low = [], []
            for s in range(slots):
                c = lax.rem(cols_ref[i, s] - me * br + br + total, total)
                c = jnp.clip(c, 0, 3 * br - 1)
                found_high.append(high[slot, c])
                found_low.append(low[slot, c])
            b_high = jnp.concatenate(found_high, axis=0)
            b_low = jnp.concatenate(found_low, axis=0)
            a = ablk[i]
            if width % 128 == 0:
                out = jnp.dot(
                    a, jnp.concatenate([b_high, b_low], axis=1), preferred_element_type=F32
                )
                p, q = out[:, :width], out[:, width:]
                result = p[:bs] + (p[bs:] + q[:bs])
            else:
                p = jnp.dot(a, b_high, preferred_element_type=F32)
                q = jnp.dot(a[:bs], b_low, preferred_element_type=F32)
                result = p[:bs] + (p[bs:] + q)
            value = (result - center * fields[step, i]) * inverse
            if step > 0:
                value = 2.0 * value - fields[step - 1, i]
            fields[step + 1, i] = value
            if step < 2:
                h, l = split(value)
                high[later, br + i] = h
                low[later, br + i] = l

    for step in range(2):
        receive(step)

        @pl.loop(0, chunks)
        def _(chunk):
            apply_chunk(step, chunk)
            for copy in halo_copies(step + 1, chunk):
                copy.start()

    share = br // bundles
    receive(2)

    def sum_copy(index, device):
        return pltpu.make_async_remote_copy(
            src_ref=sums.at[2 * index],
            dst_ref=sums.at[2 * index + 1],
            send_sem=sum_send.at[index],
            recv_sem=sum_recv.at[index],
            device_id=device,
            device_id_type=MESH,
        )

    def sum_step(index, device):
        copy = sum_copy(index, device)
        copy.start()
        copy.wait()
        sums[2 * index + 2] = sums[2 * index] + sums[2 * index + 1]

    @pl.loop(0, chunks)
    def _(chunk):
        apply_chunk(2, chunk)

    def stack_copy(index):
        target = others[index]
        return pltpu.make_async_remote_copy(
            src_ref=fields.at[3, pl.ds(target["bundle"] * share, share)],
            dst_ref=stacked_ref.at[mine],
            send_sem=all_send.at[index],
            recv_sem=all_recv.at[index],
            device_id=target,
            device_id_type=MESH,
        )

    for index in range(bundles - 1):
        stack_copy(index).start()
    stacked_ref[mine] = fields[3, pl.ds(mine * share, share)]
    for index in range(bundles - 1):
        stack_copy(index).wait_recv()
    held = [stacked_ref[b].reshape(share * bs, width) for b in range(bundles)]
    h, l = split(jnp.concatenate(held, axis=1))
    main = lax.dot_general(h, h, OVER_ROWS, preferred_element_type=F32)
    cross = lax.dot_general(h, l, OVER_ROWS, preferred_element_type=F32)
    sums[0] = main + (cross + cross.T)
    for index, device in enumerate(partners):
        sum_step(index, device)
    gram_ref[...] = sums[2 * len(partners)]
    for index in range(bundles - 1):
        stack_copy(index).wait_send()

    for step in range(3):
        @pl.loop(0, chunks)
        def _(chunk):
            for copy in halo_copies(step, chunk):
                copy.wait_send()


def paired_kernel(
    rows, cols_in, bounds_ref, vec_in, blocks_in, stacked_ref, corner_ref, diag_ref, cross_ref,
    cols_ref, vec_ref, blocks_ref, load_sem, ablk, picks, fields, halo, whole, arrived, sums, lines, halo_send, halo_recv, all_send,
    all_recv, sum_send, sum_recv,
):
    me = lax.axis_index("row")
    mine = lax.axis_index("bundle")
    theirs = 1 - mine
    br, bs = blocks_ref.shape[0], blocks_ref.shape[1]
    slots = cols_ref.shape[0]
    width = vec_ref.shape[0]
    part = width // 2
    total = br * rows
    pairs = br // 2
    chunks = CHUNKS
    per = pairs // chunks
    right = lax.rem(me + 1, rows)
    left = lax.rem(me + rows - 1, rows)
    row_bits = rows.bit_length() - 1
    partners = []
    for bit in range(row_bits):
        mask = 1 << bit
        upper = lax.rem(lax.div(me, mask), 2)
        partners.append({"row": me + mask - 2 * mask * upper})
    partners.append({"bundle": theirs})

    barrier = pltpu.get_barrier_semaphore()
    greeted = [{"row": left}, {"row": right}] + partners
    for device in greeted:
        pl.semaphore_signal(barrier, inc=1, device_id=device, device_id_type=MESH)

    loads = [
        pltpu.make_async_copy(source, target, load_sem.at[index])
        for index, (source, target) in enumerate(
            ((vec_in, vec_ref), (blocks_in, blocks_ref), (cols_in, cols_ref))
        )
    ]
    for load in loads:
        load.start()

    center = (bounds_ref[0] + bounds_ref[1]) * 0.5
    inverse = 1.0 / ((bounds_ref[1] - bounds_ref[0]) * 0.5)
    in_low = lax.broadcasted_iota(jnp.int32, (bs, width), 1) < part
    turn = lambda value: pltpu.roll(value, part, 1)

    def halo_copies(step, half, chunk):
        span = pl.ds(chunk * per, per)
        return [
            pltpu.make_async_remote_copy(
                src_ref=fields.at[half, step, span],
                dst_ref=halo.at[step, half, side, span],
                send_sem=halo_send.at[step, half, side, chunk],
                recv_sem=halo_recv.at[step, half, side, chunk],
                device_id={"row": target},
                device_id_type=MESH,
            )
            for side, target in ((0, right), (1, left))
        ]

    def keep(half, pair, value):
        h = value.astype(BF16).astype(F32)
        l = value - h
        picks[half, 2 * pair] = jnp.where(in_low, h, turn(l)).astype(BF16)
        picks[half, 2 * pair + 1] = jnp.where(in_low, turn(h), l).astype(BF16)

    def unpack(even_half, odd_half):
        return (
            jnp.where(in_low, even_half, turn(odd_half)),
            jnp.where(in_low, turn(even_half), odd_half),
        )

    loads[0].wait()
    for pair in range(pairs):
        turned = vec_ref[:, pair * 2 * bs:(pair + 1) * 2 * bs].T
        fields[0, 0, pair], fields[1, 0, pair] = unpack(turned[:bs], turned[bs:])
        if pair == per - 1:
            pl.semaphore_wait(barrier, len(greeted))
        if (pair + 1) % per == 0:
            for copy in halo_copies(0, 0, pair // per):
                copy.start()

    @pl.loop(0, chunks)
    def _(chunk):
        for copy in halo_copies(0, 1, chunk):
            copy.start()

    loads[1].wait()
    loads[2].wait()

    @pl.loop(0, br)
    def _(i):
        h, l = split(blocks_ref[i])
        ablk[i, :bs] = h
        ablk[i, bs:] = l

    def receive(step, half):
        @pl.loop(0, pairs, unroll=2)
        def _(pair):
            keep(half, pairs + pair, fields[half, step, pair])

        @pl.loop(0, chunks)
        def _(chunk):
            for side, copy in enumerate(halo_copies(step, half, chunk)):
                copy.wait_recv()
                for inner in range(per):
                    pair = chunk * per + inner
                    keep(half, side * 2 * pairs + pair, halo[step, half, side, pair])

    def apply_chunk(step, half, chunk):
        @pl.loop(0, per, unroll=per)
        def _(inner):
            pair = chunk * per + inner
            results = []
            for odd in range(2):
                i = 2 * pair + odd
                found = []
                for s in range(slots):
                    c = cols_ref[s, i] - me * br + br
                    c = jnp.where(c < 0, c + total, c)
                    c = jnp.where(c >= total, c - total, c)
                    found.append(picks[half, jnp.clip(c, 0, 3 * br - 1)])
                out = jnp.dot(ablk[i], jnp.concatenate(found, axis=0), preferred_element_type=F32)
                result = out[:bs] + out[bs:]
                results.append(result + turn(result))
            result = jnp.where(in_low, results[0], results[1])
            value = (result - center * fields[half, step, pair]) * inverse
            if step > 0:
                value = 2.0 * value - fields[half, step - 1, pair]
            fields[half, step + 1, pair] = value

    for step in range(2):
        for half in range(2):
            receive(step, half)

            @pl.loop(0, chunks)
            def _(chunk):
                apply_chunk(step, half, chunk)
                for copy in halo_copies(step + 1, half, chunk):
                    copy.start()

    share = pairs // 2
    parts = chunks // 2

    def stack_copy(half, index):
        return pltpu.make_async_remote_copy(
            src_ref=fields.at[half, 3, pl.ds(theirs * share + index * per, per)],
            dst_ref=arrived.at[half, pl.ds(index * per, per)],
            send_sem=all_send.at[half, index],
            recv_sem=all_recv.at[half, index],
            device_id={"bundle": theirs},
            device_id_type=MESH,
        )

    for half in range(2):
        receive(2, half)

        @pl.loop(0, parts)
        def _(index):
            apply_chunk(2, half, theirs * parts + index)
            stack_copy(half, index).start()

        @pl.loop(0, parts)
        def _(index):
            apply_chunk(2, half, mine * parts + index)

    @pl.loop(0, pairs, unroll=2)
    def _(pair):
        whole[2 * pair], whole[2 * pair + 1] = unpack(fields[0, 3, pair], fields[1, 3, pair])

    stacked_ref[mine] = whole[pl.ds(mine * 2 * share, 2 * share)]
    h, l = split(whole[...].reshape(br * bs, width))
    both = lax.dot_general(
        h, jnp.concatenate([h, l], axis=1), OVER_ROWS, preferred_element_type=F32
    )
    sums[0] = both[:, :width] + (both[:, width:] + both[:, width:].T)

    def sum_step(index, device, beside=None):
        copy = pltpu.make_async_remote_copy(
            src_ref=sums.at[2 * index],
            dst_ref=sums.at[2 * index + 1],
            send_sem=sum_send.at[index],
            recv_sem=sum_recv.at[index],
            device_id=device,
            device_id_type=MESH,
        )
        copy.start()
        if beside is not None:
            next(beside, None)
        copy.wait()
        sums[2 * index + 2] = sums[2 * index] + sums[2 * index + 1]

    for index in range(row_bits):
        sum_step(index, partners[index])
    done = 2 * row_bits
    diag_ref[mine] = sums[done]
    diag_copy = pltpu.make_async_remote_copy(
        src_ref=sums.at[done],
        dst_ref=diag_ref.at[mine],
        send_sem=sum_send.at[row_bits],
        recv_sem=sum_recv.at[row_bits],
        device_id={"bundle": theirs},
        device_id_type=MESH,
    )
    diag_copy.start()
    for half in range(2):
        for index in range(parts):
            stack_copy(half, index).wait_recv()

    @pl.loop(0, share, unroll=2)
    def _(pair):
        even, odd = unpack(arrived[0, pair], arrived[1, pair])
        stacked_ref[theirs, 2 * pair] = even
        stacked_ref[theirs, 2 * pair + 1] = odd

    h0, l0 = split(stacked_ref[0].reshape(2 * share * bs, width))
    h1, l1 = split(stacked_ref[1].reshape(2 * share * bs, width))
    both = lax.dot_general(
        h0, jnp.concatenate([h1, l1], axis=1), OVER_ROWS, preferred_element_type=F32
    )
    rest = lax.dot_general(l0, h1, OVER_ROWS, preferred_element_type=F32)
    sums[done + 2] = both[:, :width] + (both[:, width:] + rest)
    diag_copy.wait()
    found = []
    pieces = factor_steps(diag_ref[0], lines, found)
    for bit, device in enumerate(partners):
        sum_step(row_bits + 1 + bit, device, pieces)
    for _ in pieces:
        pass
    cross_ref[...] = sums[done + 2 + 2 * len(partners)]
    corner_ref[0], corner_ref[1] = found

    for half in range(2):
        for index in range(parts):
            stack_copy(half, index).wait_send()
        for step in range(3):
            @pl.loop(0, chunks)
            def _(chunk):
                for copy in halo_copies(step, half, chunk):
                    copy.wait_send()


def is_paired(bundles, width):
    return bundles == 2 and width == 128


def dot(a, b, dims=(((1,), (0,)), ((), ()))):
    return lax.dot_general(a, b, dims, precision=HIGHEST, preferred_element_type=F32)


def upper_part(value, lower=False):
    row = lax.broadcasted_iota(jnp.int32, value.shape, 0)
    col = lax.broadcasted_iota(jnp.int32, value.shape, 1)
    return jnp.where((col <= row) if lower else (col >= row), value, 0.0)


def factor_steps(block, lines, found):
    size = block.shape[0]
    if size > PANEL:
        half = size // 2
        part = []
        yield from factor_steps(block[:half, :half], lines, part)
        upper0, inverse0 = part
        corner = dot(inverse0, block[:half, half:])
        rest = block[half:, half:] - dot(corner, corner, OVER_ROWS)
        part = []
        yield from factor_steps(rest, lines, part)
        upper1, inverse1 = part
        side = -dot(inverse1, dot(corner, inverse0, OVER_ROWS))
        zero = jnp.zeros((half, size - half), F32)
        found.append(
            jnp.concatenate(
                [
                    jnp.concatenate([upper0, corner], axis=1),
                    jnp.concatenate([zero.T, upper1], axis=1),
                ],
                axis=0,
            )
        )
        found.append(
            jnp.concatenate(
                [
                    jnp.concatenate([inverse0, zero], axis=1),
                    jnp.concatenate([side, inverse1], axis=1),
                ],
                axis=0,
            )
        )
        return
    row = lax.broadcasted_iota(jnp.int32, (size, size), 0)
    col = lax.broadcasted_iota(jnp.int32, (size, size), 1)
    work = jnp.concatenate([block, (row == col).astype(F32)], axis=1)
    for first in range(0, size, GROUP):
        top = first // 8 * 8
        if first and first % 8 == 0:
            work = work[8:]
        index = lax.broadcasted_iota(jnp.int32, work.shape, 0)
        columns = [
            jnp.broadcast_to(work[:, first + j:first + j + 1], work.shape) for j in range(GROUP)
        ]
        for j in range(GROUP):
            at = first + j - top
            pivot = columns[j][at:at + 1]
            turned = 1.0 / pivot
            line = work[at:at + 1]
            lines[first + j:first + j + 1] = line * lax.rsqrt(pivot)
            factor = jnp.where(index > at, columns[j], 0.0)
            for m in range(j + 1, GROUP):
                columns[m] = columns[m] - factor * (columns[m][at:at + 1] * turned)
            work = work - factor * (line * turned)
        if (first + GROUP) % 32 == 0 and first + GROUP < size:
            yield
    found.append(upper_part(lines[:, :size]))
    found.append(upper_part(lines[:, size:], lower=True))
    yield


def write_basis(solver, fields, basis_ref, first):
    h, l = split(solver)
    fh, fl = split(fields)
    product = lambda a, b: lax.dot_general(a, b, OVER_LAST, preferred_element_type=F32)
    basis_ref[first:first + solver.shape[0]] = product(h, fh) + (product(h, fl) + product(l, fh))


def factor_kernel(gram_ref, stacked_ref, basis_ref, factor_ref, lines):
    found = []
    for _ in factor_steps(gram_ref[...], lines, found):
        pass
    factor_ref[...] = found[0]
    bundles, share, bs, width = stacked_ref.shape
    held = [stacked_ref[b].reshape(share * bs, width) for b in range(bundles)]
    write_basis(found[1], jnp.concatenate(held, axis=1), basis_ref, 0)


def finish_kernel(corner_ref, diag_ref, cross_ref, stacked_ref, basis_ref, factor_ref, lines):
    bundles, share, bs, width = stacked_ref.shape
    upper0, inverse0 = corner_ref[0], corner_ref[1]
    field0 = stacked_ref[0].reshape(share * bs, width)
    field1 = stacked_ref[1].reshape(share * bs, width)
    corner = dot(inverse0, cross_ref[...])
    rest = diag_ref[1] - dot(corner, corner, OVER_ROWS)
    side = dot(corner, inverse0, OVER_ROWS)
    factor_ref[:width, :width] = upper0
    factor_ref[:width, width:] = corner
    factor_ref[width:, :width] = jnp.zeros((width, width), F32)
    write_basis(inverse0, field0, basis_ref, 0)
    found = []
    for _ in factor_steps(rest, lines, found):
        pass
    upper1, inverse1 = found
    factor_ref[width:, width:] = upper1
    solver = jnp.concatenate([-dot(inverse1, side), inverse1], axis=1)
    write_basis(solver, jnp.concatenate([field0, field1], axis=1), basis_ref, width)


def solution(mesh):
    rows, bundles = mesh.shape["row"], mesh.shape["bundle"]
    row_bits, bundle_bits = rows.bit_length() - 1, bundles.bit_length() - 1
    vmem = pl.BlockSpec(memory_space=pltpu.VMEM)
    smem = pl.BlockSpec(memory_space=pltpu.SMEM)
    hbm = pl.BlockSpec(memory_space=pl.ANY)

    def local(vectors, blocks, columns, bounds):
        br, bs, wide = blocks.shape
        width = vectors.shape[0]
        count = width * bundles
        share = br // bundles
        paired = is_paired(bundles, width)
        panel = min(PANEL, width) if paired else min(PANEL, count)
        block = jax.ShapeDtypeStruct((width, width), F32)
        two = jax.ShapeDtypeStruct((2, width, width), F32)
        stack = jax.ShapeDtypeStruct((bundles, share, bs, width), F32)
        dma = pltpu.SemaphoreType.DMA
        if paired:
            sums = 2 * row_bits + 2
            kernel = functools.partial(paired_kernel, rows)
            shapes = (stack, two, two, block)
            scratch = [
                pltpu.SMEM(columns.shape[::-1], jnp.int32),
                pltpu.VMEM(vectors.shape, F32),
                pltpu.VMEM(blocks.shape, F32),
                dma((3,)),
                pltpu.VMEM((br, 2 * bs, wide), BF16),
                pltpu.VMEM((2, 3 * br, bs, width), BF16),
                pltpu.VMEM((2, 4, br // 2, bs, width), F32),
                pltpu.VMEM((3, 2, 2, br // 2, bs, width), F32),
                pltpu.VMEM((br, bs, width), F32),
                pltpu.VMEM((2, br // 4, bs, width), F32),
                pltpu.VMEM((2 * sums + 1, width, width), F32),
                pltpu.VMEM((panel, 2 * panel), F32),
                dma((3, 2, 2, CHUNKS)),
                dma((3, 2, 2, CHUNKS)),
                dma((2, CHUNKS // 2)),
                dma((2, CHUNKS // 2)),
                dma((sums,)),
                dma((sums,)),
            ]
        else:
            sums = row_bits + bundle_bits
            kernel = functools.partial(filter_kernel, rows, bundles)
            shapes = (stack, jax.ShapeDtypeStruct((count, count), F32))
            scratch = [
                pltpu.VMEM((br, 2 * bs, wide), BF16),
                pltpu.VMEM((2, 3 * br, bs, width), BF16),
                pltpu.VMEM((2, 3 * br, bs, width), BF16),
                pltpu.VMEM((4, br, bs, width), F32),
                pltpu.VMEM((3, 2, br, bs, width), F32),
                pltpu.VMEM((2 * sums + 1, count, count), F32),
                dma((3, 2, 4)),
                dma((3, 2, 4)),
                dma((max(bundles - 1, 1),)),
                dma((max(bundles - 1, 1),)),
                dma((sums,)),
                dma((sums,)),
            ]
        parts = pl.pallas_call(
            kernel,
            out_shape=shapes,
            in_specs=[hbm, smem, hbm, hbm] if paired else [smem, smem, vmem, vmem],
            out_specs=tuple(vmem for _ in shapes),
            scratch_shapes=scratch,
            compiler_params=pltpu.CompilerParams(
                collective_id=0, has_side_effects=True, vmem_limit_bytes=VMEM_LIMIT
            ),
        )(columns.T if paired else columns, bounds, vectors, blocks)
        operands = parts[1:] + parts[:1]
        return pl.pallas_call(
            finish_kernel if paired else factor_kernel,
            out_shape=(
                jax.ShapeDtypeStruct((count, share * bs), F32),
                jax.ShapeDtypeStruct((count, count), F32),
            ),
            in_specs=[vmem] * len(operands),
            out_specs=(vmem, vmem),
            scratch_shapes=[pltpu.VMEM((panel, 2 * panel), F32)],
            compiler_params=pltpu.CompilerParams(vmem_limit_bytes=VMEM_LIMIT),
        )(*operands)

    placed = (P("bundle", "row"), P("row", None, None), P("row", None), P())
    return jax.shard_map(
        local,
        mesh=mesh,
        in_specs=placed,
        out_specs=(P(None, ("row", "bundle")), P()),
        check_vma=False,
    )
```
